32 devices in a mesh: dp: 2 (over core), expert: 16 (over z, y, x).
Axes of the slice: x: 2, y: 2, z: 4, core: 2. Of those that a mesh axis runs over, the one named last changes fastest.
Arguments:
- prev_acts: bfloat16 [2, 16, 128, 3584], P('dp', 'expert'), may hold values from -6 to 6
- prev_cot: bfloat16 [2, 16, 128, 512], P('dp', 'expert'), may hold values from -0.59765625 to 0.59765625
- weights: bfloat16 [16, 3584, 512], P('expert', 'dp'), may hold values from -0.09375 to 0.09375
- first_moment: float32 [16, 3584, 512], P('expert', 'dp'), may hold values from -1.8 to 1.8
- second_moment: float32 [16, 3584, 512], P('expert', 'dp'), may hold values from 0.1 to 2
- tokens: bfloat16 [2, 16, 128, 3584], P('dp', 'expert'), may hold values from -6 to 6
- routing: int32 [2, 16, 128, 2], P('dp', 'expert'), may hold values from 0 to 3, all different within a row; in each aligned block of 128 rows (0 to 127, 128 to 255, ..., all dimensions but the last counted through in order) at most 96 rows name the same one
- gates: bfloat16 [2, 16, 128, 2], P('dp', 'expert'), may hold values from 0.19921875 to 1
- token_counts: int32 [2, 16], P('dp', 'expert'), may hold values from 64 to 128
- old_owner: int32 [4], replicated, may hold values from 0 to 3, each once
- new_owner: int32 [4], replicated, may hold values from 0 to 3, each once
Outputs:
- expert_hidden: bfloat16 [2, 16, 1536, 256], P('dp', 'expert')
- new_weights: bfloat16 [16, 3584, 512], P('expert', 'dp')
- new_first: float32 [16, 3584, 512], P('expert', 'dp')
- new_second: float32 [16, 3584, 512], P('expert', 'dp')
The draws below stay inside these ranges and needn't reach their ends.
Inputs may be any that keep to these rules, and one draw needn't show every extreme that they name: `routing`: each token names 2 different hot experts; within the rows of one device no hot expert is named by more than 96 rows. `old_owner`: each is a permutation of the 4 groups. `new_owner`: each is a permutation of the 4 groups.
All inputs are finite; a program needn't handle non-finite values.
Results may differ from the reference program's by a relative error of at most 0.013.
Values may be sent and summed in bfloat16 or wider, within the bound.
A program may use at most 128 MiB of HBM per device.

```python
import math
import jax
import jax.numpy as jnp
import numpy as np
from jax import lax

D = 3584
GRP = 4
TOPH = 2
TOK_DEV = 128
GRAD_ROWS = 128
HID = 256
HOT = 4
CAP = 96
N_DP = 2
N_EXPERT = 16


def draw_token_counts(key, part):
    count_key = jax.random.fold_in(key, 11)
    chosen_key = jax.random.fold_in(key, 12)
    counts = jax.random.randint(count_key, (N_DP * N_EXPERT,), TOK_DEV // 2, TOK_DEV + 1, dtype=jnp.int32)
    chosen = jax.random.randint(chosen_key, (), 0, N_DP * N_EXPERT, dtype=jnp.int32)
    positions = jnp.arange(N_DP * N_EXPERT, dtype=jnp.int32)
    counts = jnp.where(positions == chosen, TOK_DEV, counts)
    return counts.reshape(N_DP, N_EXPERT).astype(jnp.int32)


def draw_prev_acts(key, part):
    noise = jax.random.normal(jax.random.fold_in(key, 21), (N_DP, N_EXPERT, GRAD_ROWS, D), jnp.float32)
    values = noise
    return jnp.clip(values, -6.0, 6.0).astype(jnp.bfloat16)


def draw_tokens(key, part):
    noise = jax.random.normal(jax.random.fold_in(key, 22), (N_DP, N_EXPERT, TOK_DEV, D), jnp.float32)
    values = noise
    return jnp.clip(values, -6.0, 6.0).astype(jnp.bfloat16)


def levels(own_key, extent, shards, smallest, largest):
    gain, own = 1.0, jax.random.fold_in(own_key, 6)
    for axis_at, parts in shards:
        draws = jnp.exp(jax.random.uniform(jax.random.fold_in(own, axis_at), (parts,), jnp.float32, smallest / len(shards), largest / len(shards)))
        gain = gain * jnp.repeat(draws, extent[axis_at] // parts).reshape([-1 if axis == axis_at else 1 for axis in range(len(extent))])
    return gain


def assign_block(own_key, own, number, rows, amount, top, most, lean):
    order = jax.random.permutation(own_key, amount)
    crowded, common = load_shares(amount, rows * top, most, lean, True), load_shares(amount, rows * top, most, lean, False)
    places = jnp.arange(amount)

    def named(lengths, offset_by):
        used = int((lengths > 0).sum())
        fixed = max(1, used // 4)
        moved = fixed + (places - fixed + offset_by * (used - fixed)) % max(1, amount - fixed)
        return jnp.zeros((amount,), jnp.int32).at[order[jnp.where(places < fixed, places, moved)]].set(jnp.asarray(lengths, jnp.int32))

    lengths = jnp.where(number % 4 == 0, named(crowded, number // 4), named(common, number - number // 4 - 1))
    mixed = jax.random.permutation(jax.random.fold_in(own, 3), amount)
    source_of, receiver = mixed[0:amount // 2 * 2:2], mixed[1:amount // 2 * 2:2]
    room = jnp.minimum(lengths[source_of] - 1, most - lengths[receiver]) // 2
    room = jnp.where((source_of == order[0]) | (receiver == order[0]) | (lengths[receiver] == 0), 0, jnp.maximum(room, 0))
    moved = jax.random.randint(jax.random.fold_in(own, 4), (amount // 2,), 0, 1 << 20) % (room + 1)
    lengths = lengths.at[source_of].add(-moved).at[receiver].add(moved)
    labels = jnp.searchsorted(jnp.cumsum(lengths), jnp.arange(rows * top), side="right").astype(jnp.int32)
    table = labels.reshape(top, rows).T
    table = table[jax.random.permutation(jax.random.fold_in(own, 1), rows)]
    offset_by = jax.random.randint(jax.random.fold_in(own, 2), (rows, 1), 0, top)
    return jnp.take_along_axis(table, (jnp.arange(top)[None, :] + offset_by) % top, axis=1)


def load_shares(number_of, total, most, lean, full):
    loads = [(1 << 20) // math.isqrt(grade ** lean) + 1 for grade in range(1, number_of + 1)]
    largest = most if full else min(most, max(-(-total // number_of), total * loads[0] // sum(loads)))
    least = 1 if total - largest >= number_of - 1 else 0
    given, spare = [largest] + [least] * (number_of - 1), total - largest - least * (number_of - 1)
    while spare > 0:
        candidates = [i for i in range(1, number_of) if given[i] < largest] or [i for i in range(1, number_of) if given[i] < most]
        pool, remaining = sum([loads[i] for i in candidates]), spare
        for i in candidates:
            extra = min(most - given[i], max(1, remaining * loads[i] // pool), spare)
            given[i] = given[i] + extra
            spare = spare - extra
    return np.array(given)


def centred(rng, extent, deviation, most, split=(), held_as=jnp.bfloat16):
    array = jax.random.normal(rng, extent, jnp.float32) * deviation
    if len(split) > 0:
        array = levels(rng, extent, split, -0.22, 0.18) * array
    return jnp.clip(array, min=-most, max=most).astype(held_as)


def setup_inputs(seed: int = 0) -> dict:
    splits = jax.random.split(jax.random.key(seed), 12)
    prev_acts = draw_prev_acts(jax.random.fold_in(splits[11], 71), 0)
    prev_cot = centred(splits[1], (N_DP, N_EXPERT, GRAD_ROWS, 2 * HID), 0.1, 0.59765625, ((0, 2), (1, 16)))
    weights = centred(splits[2], (N_EXPERT, D, 2 * HID), D ** -0.5, 0.09375, ((0, 16), (1, 2)))
    first_moment = centred(splits[3], (N_EXPERT, D, 2 * HID), 0.3, 1.8, ((0, 16), (1, 2)), jnp.float32)
    second_moment = jnp.clip(jnp.exp(math.log(2.0) - 2.9957323 * jax.random.uniform(splits[4], (N_EXPERT, D, 2 * HID), jnp.float32) ** levels(splits[4], (N_EXPERT, D, 2 * HID), ((0, 16), (1, 2)), -0.2, 0.2)), 0.1, 2.0)
    tokens = draw_tokens(jax.random.fold_in(splits[11], 71), 0)
    routing_keys = jax.random.split(jax.random.fold_in(splits[6], 1), N_DP * N_EXPERT * TOK_DEV // TOK_DEV)
    routing_turns = jax.random.permutation(jax.random.fold_in(splits[6], 3), N_DP * N_EXPERT * TOK_DEV // TOK_DEV)
    routing = jax.vmap(lambda own, number: assign_block(jax.random.fold_in(splits[6], 2), own, number, TOK_DEV, HOT, TOPH, CAP, 2))(routing_keys, routing_turns).reshape((N_DP, N_EXPERT, TOK_DEV, TOPH))
    gates = jnp.clip(0.19921875 + 0.80078125 * jax.random.uniform(splits[7], (N_DP, N_EXPERT, TOK_DEV, TOPH), jnp.float32) ** levels(splits[7], (N_DP, N_EXPERT, TOK_DEV, TOPH), ((0, 2), (1, 16)), -0.2, 0.2), 0.19921875, 1.0).astype(jnp.bfloat16)
    token_counts = draw_token_counts(jax.random.fold_in(splits[11], 71), 0)
    old_owner = jax.random.permutation(splits[9], HOT).astype(jnp.int32)
    new_owner = jax.random.permutation(splits[10], HOT).astype(jnp.int32)
    return {"prev_acts": prev_acts, "prev_cot": prev_cot, "weights": weights, "first_moment": first_moment, "second_moment": second_moment, "tokens": tokens, "routing": routing, "gates": gates, "token_counts": token_counts, "old_owner": old_owner, "new_owner": new_owner}


beta_first = 0.9
beta_second = 0.95
learning = 0.00022
decay_rate = 0.1
epsilon = 1e-08
first_fix = 1.0 - 0.9 ** 40
second_fix = 1.0 - 0.95 ** 40

def adamw(weight_now, first_now, second_now, gradient):
    first_next = beta_first * first_now + (1.0 - beta_first) * gradient
    second_next = beta_second * second_now + (1.0 - beta_second) * gradient * gradient
    stepped = weight_now.astype(jnp.float32) * (1.0 - learning * decay_rate) - learning * (first_next / first_fix) / (jnp.sqrt(second_next / second_fix) + epsilon)
    return (stepped.astype(jnp.bfloat16), first_next, second_next)

def pack_tokens(token_block, route_block, gate_block, limit):
    hot_index = jnp.arange(HOT, dtype=jnp.int32)
    valid = jnp.arange(token_block.shape[0], dtype=jnp.int32) < limit
    hits = (route_block[:, :, None] == hot_index[None, None, :]) & valid[:, None, None]
    named = lax.optimization_barrier(jnp.sum(hits.astype(jnp.int32), axis=1)).astype(jnp.int32)
    scales = lax.optimization_barrier(jnp.sum(jnp.where(hits, gate_block.astype(jnp.float32)[:, :, None], 0.0), axis=1))
    ranks = (jnp.cumsum(named, axis=0) - named).astype(jnp.int32)
    slots = jnp.arange(CAP, dtype=jnp.int32)
    placed = (ranks.T[:, None, :] == slots[None, :, None]) & (named.T[:, None, :] == 1)
    packed = jnp.einsum('hct,td->hcd', placed.astype(jnp.float32), token_block.astype(jnp.float32)).astype(jnp.bfloat16)
    gate_scale = jnp.einsum('hct,th->hc', placed.astype(jnp.float32), scales).astype(jnp.bfloat16)
    return (packed, gate_scale)

def reference(prev_acts, prev_cot, weights, first_moment, second_moment, tokens, routing, gates, token_counts, old_owner, new_owner):
    hot_index = jnp.arange(HOT, dtype=jnp.int32)
    holder = lax.optimization_barrier(jnp.sum(jnp.where(new_owner[None, :] == hot_index[:, None], hot_index[None, :], 0), axis=1)).astype(jnp.int32)
    owners = jnp.arange(N_EXPERT, dtype=jnp.int32)
    source = (jnp.take(old_owner, jnp.take(holder, owners // GRP)) * GRP + owners % GRP).astype(jnp.int32)

    def update(expert):
        running = jnp.zeros((D, 2 * HID), jnp.float32)
        for replica in range(N_DP):
            term = jnp.dot(prev_acts[replica, expert].T, prev_cot[replica, expert], preferred_element_type=jnp.float32)
            running = running + lax.optimization_barrier(term.astype(jnp.bfloat16)).astype(jnp.float32)
        return adamw(weights[expert], first_moment[expert], second_moment[expert], running)
    updated, first_next, second_next = lax.map(update, owners)
    new_weights = jnp.take(updated, source, axis=0)
    new_first = jnp.take(first_next, source, axis=0)
    new_second = jnp.take(second_next, source, axis=0)

    def pack_one(flat_index):
        replica = flat_index // N_EXPERT
        expert = flat_index % N_EXPERT
        return pack_tokens(tokens[replica, expert], routing[replica, expert], gates[replica, expert], token_counts[replica, expert])
    packed, gate_scale = lax.map(pack_one, jnp.arange(N_DP * N_EXPERT, dtype=jnp.int32))
    packed = packed.reshape(N_DP, N_EXPERT, HOT, CAP, D)
    gate_scale = gate_scale.reshape(N_DP, N_EXPERT, HOT, CAP)

    def serve(flat_index):
        replica = flat_index // N_EXPERT
        expert = flat_index % N_EXPERT
        chosen = holder[expert // GRP]
        received = packed[replica][:, chosen].reshape(N_EXPERT * CAP, D)
        scaling = gate_scale[replica][:, chosen].reshape(N_EXPERT * CAP)
        projected = jnp.dot(received, new_weights[expert], preferred_element_type=jnp.float32)
        result = jax.nn.silu(projected[:, :HID]) * projected[:, HID:] * scaling.astype(jnp.float32)[:, None]
        return result.astype(jnp.bfloat16)
    hidden = lax.map(serve, jnp.arange(N_DP * N_EXPERT, dtype=jnp.int32))
    hidden = hidden.reshape(N_DP, N_EXPERT, N_EXPERT * CAP, HID)
    return (hidden, new_weights, new_first, new_second)
```

```python
import itertools

import jax
import jax.numpy as jnp
import numpy as np
from jax import lax
from jax.sharding import PartitionSpec as P

D = 3584
GRP = 4


beta_first = 0.9
beta_second = 0.95
learning = 0.00022
decay_rate = 0.1
epsilon = 1e-08
first_fix = 1.0 - 0.9**40
second_fix = 1.0 - 0.95**40


def adamw(weight_now, first_now, second_now, gradient):
    first_next = beta_first * first_now + (1.0 - beta_first) * gradient
    second_next = beta_second * second_now + (1.0 - beta_second) * gradient * gradient
    stepped = weight_now.astype(jnp.float32) * (1.0 - learning * decay_rate) - learning * (
        first_next / first_fix
    ) / (jnp.sqrt(second_next / second_fix) + epsilon)
    return stepped.astype(jnp.bfloat16), first_next, second_next


def migrate_spread(arrays, source, experts):
    moved = []
    for array in arrays:
        split = array.reshape(experts, array.shape[0] // experts, array.shape[1])
        spread = lax.all_to_all(split, "expert", split_axis=0, concat_axis=0, tiled=True)
        ordered = jnp.take(spread, source, axis=0)
        home = lax.all_to_all(ordered, "expert", split_axis=0, concat_axis=0, tiled=True)
        moved.append(home.reshape(array.shape))
    return moved


def pack_tokens(token_block, route_block, gate_block, limit, wanted, capacity):
    valid = jnp.arange(token_block.shape[0], dtype=jnp.int32) < limit
    hits = (route_block[:, :, None] == wanted[None, None, :]) & valid[:, None, None]
    named = jnp.sum(hits.astype(jnp.int32), axis=1)
    scales = jnp.sum(jnp.where(hits, gate_block.astype(jnp.float32)[:, :, None], 0.0), axis=1)
    ranks = jnp.cumsum(named, axis=0) - named
    slots = jnp.arange(capacity, dtype=jnp.int32)
    placed = (ranks.T[:, None, :] == slots[None, :, None]) & (named.T[:, None, :] == 1)
    scale = jnp.sum(jnp.where(placed, scales.T[:, None, :], 0.0), axis=2).astype(jnp.bfloat16)
    return placed.astype(jnp.bfloat16), scale


def exchange(array, experts, flip):
    return lax.ppermute(array, "expert", [(e, e ^ flip) for e in range(experts)])


def dispatch(packed, experts):
    blocks = []
    for step in range(experts // GRP):
        own = packed[step]
        if step:
            own = exchange(own, experts, step * GRP)
        first, second = (1, 2) if step % 2 == 0 else (2, 1)
        near = exchange(own, experts, first)
        side = exchange(own, experts, second)
        far = exchange(near, experts, second)
        row = {0: own, first: near, second: side, 3: far}
        blocks.append([row[k] for k in range(GRP)])
    return blocks


def both_halves(mine, dp_size):
    if dp_size != 2:
        return lax.all_gather(mine, "dp", axis=0, tiled=True)
    other = lax.ppermute(mine, "dp", [(0, 1), (1, 0)])
    low = lax.axis_index("dp") == 0
    return jnp.concatenate([jnp.where(low, mine, other), jnp.where(low, other, mine)], axis=0)


def dot_t(acts, cot):
    return lax.dot_general(
        acts, cot, (((0,), (0,)), ((), ())), preferred_element_type=jnp.float32
    ).astype(jnp.bfloat16)


def summed_grads(acts, cot, rows_dev, dp_size):
    if dp_size != 2:
        return lax.psum_scatter(
            dot_t(acts, cot), "dp", scatter_dimension=0, tiled=True
        ).astype(jnp.float32)
    me = lax.axis_index("dp")
    theirs = dot_t(lax.dynamic_slice_in_dim(acts, (1 - me) * rows_dev, rows_dev, 1), cot)
    arrived = lax.ppermute(theirs, "dp", [(0, 1), (1, 0)])
    ours = dot_t(lax.dynamic_slice_in_dim(acts, me * rows_dev, rows_dev, 1), cot)
    return ours.astype(jnp.float32) + arrived.astype(jnp.float32)


def local(
    prev_acts,
    prev_cot,
    weights,
    first_moment,
    second_moment,
    tokens,
    routing,
    gates,
    token_counts,
    old_owner,
    new_owner,
):
    experts = lax.axis_size("expert")
    dp_size = lax.axis_size("dp")
    groups = experts // GRP
    token_slots = tokens.shape[2]
    capacity = min(token_slots, 3 * token_slots // groups)
    rows_dev, width = weights.shape[1:]
    hidden_units = width // 2
    hot_index = jnp.arange(groups, dtype=jnp.int32)
    holder = jnp.sum(
        jnp.where(new_owner[None, :] == hot_index[:, None], hot_index[None, :], 0), axis=1
    )
    came_from = jnp.take(old_owner, holder)
    my_group = lax.axis_index("expert") // GRP
    my_place = lax.axis_index("expert") % GRP

    placed, scale = pack_tokens(
        tokens[0, 0], routing[0, 0], gates[0, 0], token_counts[0, 0], holder, capacity
    )
    scale_all = lax.all_gather(scale, "expert", axis=0)
    scale_in = lax.dynamic_index_in_dim(scale_all, my_group, 1, keepdims=False)

    def finish(move, placed, scale_in, tokens, prev_acts, prev_cot, weights, first_moment, second_moment):
        packed = [
            jnp.dot(
                lax.dynamic_index_in_dim(placed, my_group ^ step, 0, keepdims=False),
                tokens[0, 0],
                preferred_element_type=jnp.float32,
            ).astype(jnp.bfloat16)
            for step in range(groups)
        ]
        blocks = dispatch(packed, experts)
        grads = summed_grads(prev_acts[0, 0], prev_cot[0, 0], rows_dev, dp_size)
        stepped, first_next, second_next = adamw(
            weights[0], first_moment[0], second_moment[0], grads
        )
        new_weight, new_first, new_second = move(stepped, first_next, second_next)
        full = both_halves(new_weight, dp_size)
        projected = jnp.stack(
            [
                jnp.dot(
                    jnp.concatenate(row, axis=0), full, preferred_element_type=jnp.float32
                ).reshape(GRP, capacity, width)
                for row in blocks
            ]
        )
        owners = jnp.arange(experts, dtype=jnp.int32)
        relative = owners ^ (my_group * GRP + my_place)
        projected = jnp.take(projected.reshape(experts, capacity, width), relative, axis=0)
        result = (
            jax.nn.silu(projected[..., :hidden_units])
            * projected[..., hidden_units:]
            * scale_in.astype(jnp.float32)[:, :, None]
        )
        hidden = result.astype(jnp.bfloat16).reshape(1, 1, experts * capacity, hidden_units)
        return hidden, new_weight[None], new_first[None], new_second[None]

    operands = (placed, scale_in, tokens, prev_acts, prev_cot, weights, first_moment, second_moment)
    if groups > 4:
        owners = jnp.arange(experts, dtype=jnp.int32)
        source = jnp.take(came_from, owners // GRP) * GRP + owners % GRP

        def move(*arrays):
            halves = [array.astype(jnp.bfloat16) for array in arrays]
            moved = migrate_spread(halves, source, experts)
            return [m.astype(array.dtype) for m, array in zip(moved, arrays)]

        return finish(move, *operands)

    orders = list(itertools.permutations(range(groups)))

    def branch(order):
        pairs = [(order[e // GRP] * GRP + e % GRP, e) for e in range(experts)]

        def move(*arrays):
            if order == tuple(range(groups)):
                return arrays
            return [
                lax.ppermute(array.astype(jnp.bfloat16), "expert", pairs).astype(array.dtype)
                for array in arrays
            ]

        return lambda *operands: finish(move, *operands)

    table = jnp.asarray(np.array(orders, np.int32))
    same = jnp.all(table == came_from[None, :], axis=1)
    chosen = jnp.sum(jnp.where(same, jnp.arange(len(orders), dtype=jnp.int32), 0))
    return lax.switch(chosen, [branch(order) for order in orders], *operands)


def solution(mesh):
    in_specs = (
        P("dp", "expert", None, None),
        P("dp", "expert", None, None),
        P("expert", "dp", None),
        P("expert", "dp", None),
        P("expert", "dp", None),
        P("dp", "expert", None, None),
        P("dp", "expert", None, None),
        P("dp", "expert", None, None),
        P("dp", "expert"),
        P(),
        P(),
    )
    out_specs = (
        P("dp", "expert", None, None),
        P("expert", "dp", None),
        P("expert", "dp", None),
        P("expert", "dp", None),
    )
    return jax.shard_map(local, mesh=mesh, in_specs=in_specs, out_specs=out_specs, check_vma=False)
```

```python
import itertools

import jax
import jax.numpy as jnp
import numpy as np
from jax import lax
from jax.sharding import PartitionSpec as P

D = 3584
GRP = 4
LANES = 128


beta_first = 0.9
beta_second = 0.95
learning = 0.00022
decay_rate = 0.1
epsilon = 1e-08
first_fix = 1.0 - 0.9**40
second_fix = 1.0 - 0.95**40


def adamw(weight_now, first_now, second_now, gradient):
    first_next = beta_first * first_now + (1.0 - beta_first) * gradient
    second_next = beta_second * second_now + (1.0 - beta_second) * gradient * gradient
    stepped = weight_now.astype(jnp.float32) * (1.0 - learning * decay_rate) - learning * (
        first_next / first_fix
    ) / (jnp.sqrt(second_next / second_fix) + epsilon)
    return stepped.astype(jnp.bfloat16), first_next, second_next


def migrate_spread(arrays, source, experts):
    moved = []
    for array in arrays:
        split = array.reshape(experts, array.shape[0] // experts, array.shape[1])
        spread = lax.all_to_all(split, "expert", split_axis=0, concat_axis=0, tiled=True)
        ordered = jnp.take(spread, source, axis=0)
        home = lax.all_to_all(ordered, "expert", split_axis=0, concat_axis=0, tiled=True)
        moved.append(home.reshape(array.shape))
    return moved


def pack_tokens(token_block, route_block, gate_block, limit, wanted, capacity):
    valid = jnp.arange(token_block.shape[0], dtype=jnp.int32) < limit
    hits = (route_block[:, :, None] == wanted[None, None, :]) & valid[:, None, None]
    named = jnp.sum(hits.astype(jnp.int32), axis=1)
    scales = jnp.sum(jnp.where(hits, gate_block.astype(jnp.float32)[:, :, None], 0.0), axis=1)
    order = jnp.arange(token_block.shape[0], dtype=jnp.int32)
    earlier = (order[None, :] < order[:, None]).astype(jnp.bfloat16)
    ranks = jnp.dot(
        earlier, named.astype(jnp.bfloat16), preferred_element_type=jnp.float32
    ).astype(jnp.int32)
    slots = jnp.arange(capacity, dtype=jnp.int32)
    placed = (ranks.T[:, None, :] == slots[None, :, None]) & (named.T[:, None, :] == 1)
    scale = jnp.sum(jnp.where(placed, scales.T[:, None, :], 0.0), axis=2).astype(jnp.bfloat16)
    return placed.astype(jnp.bfloat16), scale


def exchange(array, experts, flip):
    return lax.ppermute(array, "expert", [(e, e ^ flip) for e in range(experts)])


def spread_in_plane(received, experts):
    blocks = []
    for step, own in enumerate(received):
        first, second = (1, 2) if step % 2 == 0 else (2, 1)
        near = exchange(own, experts, first)
        side = exchange(own, experts, second)
        far = exchange(near, experts, second)
        row = {0: own, first: near, second: side, 3: far}
        blocks.append([row[k] for k in range(GRP)])
    return blocks


def both_halves(mine, dp_size):
    if dp_size != 2:
        return lax.all_gather(mine, "dp", axis=0, tiled=True)
    other = lax.ppermute(mine, "dp", [(0, 1), (1, 0)])
    low = lax.axis_index("dp") == 0
    return jnp.concatenate([jnp.where(low, mine, other), jnp.where(low, other, mine)], axis=0)


def dot_t(acts, cot):
    return lax.dot_general(
        acts, cot, (((0,), (0,)), ((), ())), preferred_element_type=jnp.float32
    ).astype(jnp.bfloat16)


def summed_grads(acts, cot, rows_dev, dp_size):
    if dp_size != 2:
        return lax.psum_scatter(
            dot_t(acts, cot), "dp", scatter_dimension=0, tiled=True
        ).astype(jnp.float32)
    me = lax.axis_index("dp")
    theirs = dot_t(lax.dynamic_slice_in_dim(acts, (1 - me) * rows_dev, rows_dev, 1), cot)
    arrived = lax.ppermute(theirs, "dp", [(0, 1), (1, 0)])
    ours = dot_t(lax.dynamic_slice_in_dim(acts, me * rows_dev, rows_dev, 1), cot)
    return ours.astype(jnp.float32) + arrived.astype(jnp.float32)


def local(
    prev_acts,
    prev_cot,
    weights,
    first_moment,
    second_moment,
    tokens,
    routing,
    gates,
    token_counts,
    old_owner,
    new_owner,
):
    experts = lax.axis_size("expert")
    dp_size = lax.axis_size("dp")
    groups = experts // GRP
    token_slots = tokens.shape[2]
    capacity = min(token_slots, 3 * token_slots // groups)
    rows_dev, width = weights.shape[1:]
    hidden_units = width // 2
    hot_index = jnp.arange(groups, dtype=jnp.int32)
    holder = jnp.sum(
        jnp.where(new_owner[None, :] == hot_index[:, None], hot_index[None, :], 0), axis=1
    )
    came_from = jnp.take(old_owner, holder)
    my_group = lax.axis_index("expert") // GRP
    my_place = lax.axis_index("expert") % GRP

    placed, scale = pack_tokens(
        tokens[0, 0], routing[0, 0], gates[0, 0], token_counts[0, 0], holder, capacity
    )

    def finish(move, placed, scale, tokens, prev_acts, prev_cot, weights, first_moment, second_moment):
        received = []
        for step in range(groups):
            put = lax.dynamic_index_in_dim(placed, my_group ^ step, 0, keepdims=False)
            gate = lax.dynamic_index_in_dim(scale, my_group ^ step, 0, keepdims=False)
            rows = jnp.dot(put, tokens[0, 0], preferred_element_type=jnp.float32)
            packed = jnp.concatenate(
                [
                    rows.astype(jnp.bfloat16),
                    jnp.broadcast_to(gate[:, None], (capacity, LANES)),
                ],
                axis=1,
            )
            received.append(exchange(packed, experts, step * GRP) if step else packed)
        grads = summed_grads(prev_acts[0, 0], prev_cot[0, 0], rows_dev, dp_size)
        stepped, first_next, second_next = adamw(
            weights[0], first_moment[0], second_moment[0], grads
        )
        (new_weight,) = move(stepped)
        first_sent, second_sent, *received[1:] = lax.optimization_barrier(
            (first_next.astype(jnp.bfloat16), second_next.astype(jnp.bfloat16), *received[1:])
        )
        new_first, new_second = (
            array.astype(jnp.float32) for array in move(first_sent, second_sent)
        )
        blocks = spread_in_plane(received, experts)
        full = jnp.concatenate(
            [both_halves(new_weight, dp_size), jnp.zeros((LANES, width), jnp.bfloat16)], axis=0
        )
        pieces, scales = [], []
        for row in blocks:
            rows = jnp.concatenate(row, axis=0)
            piece = jnp.dot(rows, full, preferred_element_type=jnp.float32)
            pieces.append(piece.reshape(GRP, capacity, width))
            scales.append(rows[:, D].reshape(GRP, capacity))
        projected, scale_in = jnp.stack(pieces), jnp.stack(scales)
        owners = jnp.arange(experts, dtype=jnp.int32)
        relative = owners ^ (my_group * GRP + my_place)
        projected = jnp.take(projected.reshape(experts, capacity, width), relative, axis=0)
        scale_in = jnp.take(scale_in.reshape(experts, capacity), relative, axis=0)
        result = (
            jax.nn.silu(projected[..., :hidden_units])
            * projected[..., hidden_units:]
            * scale_in.astype(jnp.float32)[:, :, None]
        )
        hidden = result.astype(jnp.bfloat16).reshape(1, 1, experts * capacity, hidden_units)
        return hidden, new_weight[None], new_first[None], new_second[None]

    operands = (placed, scale, tokens, prev_acts, prev_cot, weights, first_moment, second_moment)
    if groups > 4:
        owners = jnp.arange(experts, dtype=jnp.int32)
        source = jnp.take(came_from, owners // GRP) * GRP + owners % GRP

        def move(*arrays):
            return migrate_spread(arrays, source, experts)

        return finish(move, *operands)

    orders = list(itertools.permutations(range(groups)))

    def branch(order):
        pairs = [(order[e // GRP] * GRP + e % GRP, e) for e in range(experts)]

        def move(*arrays):
            if order == tuple(range(groups)):
                return arrays
            return [lax.ppermute(array, "expert", pairs) for array in arrays]

        return lambda *operands: finish(move, *operands)

    table = jnp.asarray(np.array(orders, np.int32))
    same = jnp.all(table == came_from[None, :], axis=1)
    chosen = jnp.sum(jnp.where(same, jnp.arange(len(orders), dtype=jnp.int32), 0))
    return lax.switch(chosen, [branch(order) for order in orders], *operands)


def solution(mesh):
    in_specs = (
        P("dp", "expert", None, None),
        P("dp", "expert", None, None),
        P("expert", "dp", None),
        P("expert", "dp", None),
        P("expert", "dp", None),
        P("dp", "expert", None, None),
        P("dp", "expert", None, None),
        P("dp", "expert", None, None),
        P("dp", "expert"),
        P(),
        P(),
    )
    out_specs = (
        P("dp", "expert", None, None),
        P("expert", "dp", None),
        P("expert", "dp", None),
        P("expert", "dp", None),
    )
    return jax.shard_map(local, mesh=mesh, in_specs=in_specs, out_specs=out_specs, check_vma=False)
```

```python
import itertools

import jax
import jax.numpy as jnp
import numpy as np
from jax import lax
from jax.sharding import PartitionSpec as P

D = 3584
GRP = 4
LANES = 128


beta_first = 0.9
beta_second = 0.95
learning = 0.00022
decay_rate = 0.1
epsilon = 1e-08
first_fix = 1.0 - 0.9**40
second_fix = 1.0 - 0.95**40


def adamw(weight_now, first_now, second_now, gradient):
    first_next = beta_first * first_now + (1.0 - beta_first) * gradient
    second_next = beta_second * second_now + (1.0 - beta_second) * gradient * gradient
    stepped = weight_now.astype(jnp.float32) * (1.0 - learning * decay_rate) - learning * (
        first_next / first_fix
    ) / (jnp.sqrt(second_next / second_fix) + epsilon)
    return stepped.astype(jnp.bfloat16), first_next, second_next


def migrate_spread(arrays, source, experts):
    moved = []
    for array in arrays:
        split = array.reshape(experts, array.shape[0] // experts, array.shape[1])
        spread = lax.all_to_all(split, "expert", split_axis=0, concat_axis=0, tiled=True)
        ordered = jnp.take(spread, source, axis=0)
        home = lax.all_to_all(ordered, "expert", split_axis=0, concat_axis=0, tiled=True)
        moved.append(home.reshape(array.shape))
    return moved


def pack_tokens(token_block, route_block, gate_block, limit, wanted, capacity):
    valid = jnp.arange(token_block.shape[0], dtype=jnp.int32) < limit
    hits = (route_block[:, :, None] == wanted[None, None, :]) & valid[:, None, None]
    named = jnp.sum(hits.astype(jnp.int32), axis=1)
    scales = jnp.sum(jnp.where(hits, gate_block.astype(jnp.float32)[:, :, None], 0.0), axis=1)
    order = jnp.arange(token_block.shape[0], dtype=jnp.int32)
    earlier = (order[None, :] < order[:, None]).astype(jnp.bfloat16)
    ranks = jnp.dot(
        earlier, named.astype(jnp.bfloat16), preferred_element_type=jnp.float32
    ).astype(jnp.int32)
    slots = jnp.arange(capacity, dtype=jnp.int32)
    placed = (ranks.T[:, None, :] == slots[None, :, None]) & (named.T[:, None, :] == 1)
    scale = jnp.sum(jnp.where(placed, scales.T[:, None, :], 0.0), axis=2).astype(jnp.bfloat16)
    return placed.astype(jnp.bfloat16), scale


def exchange(array, experts, flip):
    return lax.ppermute(array, "expert", [(e, e ^ flip) for e in range(experts)])


def spread_in_plane(received, experts):
    blocks = []
    for step, own in enumerate(received):
        first, second = (1, 2) if step % 2 == 0 else (2, 1)
        near = exchange(own, experts, first)
        side = exchange(own, experts, second)
        far = exchange(near, experts, second)
        row = {0: own, first: near, second: side, 3: far}
        blocks.append([row[k] for k in range(GRP)])
    return blocks


def both_halves(mine, dp_size):
    if dp_size != 2:
        return lax.all_gather(mine, "dp", axis=0, tiled=True)
    other = lax.ppermute(mine, "dp", [(0, 1), (1, 0)])
    low = lax.axis_index("dp") == 0
    return jnp.concatenate([jnp.where(low, mine, other), jnp.where(low, other, mine)], axis=0)


def dot_t(acts, cot):
    return lax.dot_general(
        acts, cot, (((0,), (0,)), ((), ())), preferred_element_type=jnp.float32
    ).astype(jnp.bfloat16)


def summed_grads(acts, cot, rows_dev, dp_size):
    if dp_size != 2:
        return lax.psum_scatter(
            dot_t(acts, cot), "dp", scatter_dimension=0, tiled=True
        ).astype(jnp.float32)
    me = lax.axis_index("dp")
    theirs = dot_t(lax.dynamic_slice_in_dim(acts, (1 - me) * rows_dev, rows_dev, 1), cot)
    arrived = lax.ppermute(theirs, "dp", [(0, 1), (1, 0)])
    ours = dot_t(lax.dynamic_slice_in_dim(acts, me * rows_dev, rows_dev, 1), cot)
    return ours.astype(jnp.float32) + arrived.astype(jnp.float32)


def local(
    prev_acts,
    prev_cot,
    weights,
    first_moment,
    second_moment,
    tokens,
    routing,
    gates,
    token_counts,
    old_owner,
    new_owner,
):
    experts = lax.axis_size("expert")
    dp_size = lax.axis_size("dp")
    groups = experts // GRP
    token_slots = tokens.shape[2]
    capacity = min(token_slots, 3 * token_slots // groups)
    rows_dev, width = weights.shape[1:]
    hidden_units = width // 2
    hot_index = jnp.arange(groups, dtype=jnp.int32)
    holder = jnp.sum(
        jnp.where(new_owner[None, :] == hot_index[:, None], hot_index[None, :], 0), axis=1
    )
    came_from = jnp.take(old_owner, holder)
    my_group = lax.axis_index("expert") // GRP
    my_place = lax.axis_index("expert") % GRP

    placed, scale = pack_tokens(
        tokens[0, 0], routing[0, 0], gates[0, 0], token_counts[0, 0], holder, capacity
    )

    def finish(move, placed, scale, tokens, prev_acts, prev_cot, weights, first_moment, second_moment):
        received = []
        for step in range(groups):
            put = lax.dynamic_index_in_dim(placed, my_group ^ step, 0, keepdims=False)
            gate = lax.dynamic_index_in_dim(scale, my_group ^ step, 0, keepdims=False)
            rows = jnp.dot(put, tokens[0, 0], preferred_element_type=jnp.float32)
            packed = jnp.concatenate(
                [
                    rows.astype(jnp.bfloat16),
                    jnp.broadcast_to(gate[:, None], (capacity, LANES)),
                ],
                axis=1,
            )
            received.append(exchange(packed, experts, step * GRP) if step else packed)
        grads = summed_grads(prev_acts[0, 0], prev_cot[0, 0], rows_dev, dp_size)
        stepped, first_next, second_next = adamw(
            weights[0], first_moment[0], second_moment[0], grads
        )
        (new_weight,) = move(stepped)
        second_sent, *received[1:] = lax.optimization_barrier(
            (second_next.astype(jnp.bfloat16), *received[1:])
        )
        new_first, new_second = (
            array.astype(jnp.float32)
            for array in move(first_next.astype(jnp.bfloat16), second_sent)
        )
        blocks = spread_in_plane(received, experts)
        full = jnp.concatenate(
            [both_halves(new_weight, dp_size), jnp.zeros((LANES, width), jnp.bfloat16)], axis=0
        )
        pieces, scales = [], []
        for row in blocks:
            rows = jnp.concatenate(row, axis=0)
            piece = jnp.dot(rows, full, preferred_element_type=jnp.float32)
            pieces.append(piece.reshape(GRP, capacity, width))
            scales.append(rows[:, D].reshape(GRP, capacity))
        projected, scale_in = jnp.stack(pieces), jnp.stack(scales)
        owners = jnp.arange(experts, dtype=jnp.int32)
        relative = owners ^ (my_group * GRP + my_place)
        projected = jnp.take(projected.reshape(experts, capacity, width), relative, axis=0)
        scale_in = jnp.take(scale_in.reshape(experts, capacity), relative, axis=0)
        result = (
            jax.nn.silu(projected[..., :hidden_units])
            * projected[..., hidden_units:]
            * scale_in.astype(jnp.float32)[:, :, None]
        )
        hidden = result.astype(jnp.bfloat16).reshape(1, 1, experts * capacity, hidden_units)
        return hidden, new_weight[None], new_first[None], new_second[None]

    operands = (placed, scale, tokens, prev_acts, prev_cot, weights, first_moment, second_moment)
    if groups > 4:
        owners = jnp.arange(experts, dtype=jnp.int32)
        source = jnp.take(came_from, owners // GRP) * GRP + owners % GRP

        def move(*arrays):
            return migrate_spread(arrays, source, experts)

        return finish(move, *operands)

    orders = list(itertools.permutations(range(groups)))

    def branch(order):
        pairs = [(order[e // GRP] * GRP + e % GRP, e) for e in range(experts)]

        def move(*arrays):
            if order == tuple(range(groups)):
                return arrays
            return [lax.ppermute(array, "expert", pairs) for array in arrays]

        return lambda *operands: finish(move, *operands)

    table = jnp.asarray(np.array(orders, np.int32))
    same = jnp.all(table == came_from[None, :], axis=1)
    chosen = jnp.sum(jnp.where(same, jnp.arange(len(orders), dtype=jnp.int32), 0))
    return lax.switch(chosen, [branch(order) for order in orders], *operands)


def solution(mesh):
    in_specs = (
        P("dp", "expert", None, None),
        P("dp", "expert", None, None),
        P("expert", "dp", None),
        P("expert", "dp", None),
        P("expert", "dp", None),
        P("dp", "expert", None, None),
        P("dp", "expert", None, None),
        P("dp", "expert", None, None),
        P("dp", "expert"),
        P(),
        P(),
    )
    out_specs = (
        P("dp", "expert", None, None),
        P("expert", "dp", None),
        P("expert", "dp", None),
        P("expert", "dp", None),
    )
    return jax.shard_map(local, mesh=mesh, in_specs=in_specs, out_specs=out_specs, check_vma=False)
```

```python
import itertools

import jax
import jax.numpy as jnp
import numpy as np
from jax import lax
from jax.sharding import PartitionSpec as P

D = 3584
GRP = 4
LANES = 128


beta_first = 0.9
beta_second = 0.95
learning = 0.00022
decay_rate = 0.1
epsilon = 1e-08
first_fix = 1.0 - 0.9**40
second_fix = 1.0 - 0.95**40


def adamw(weight_now, first_now, second_now, gradient):
    first_next = beta_first * first_now + (1.0 - beta_first) * gradient
    second_next = beta_second * second_now + (1.0 - beta_second) * gradient * gradient
    stepped = weight_now.astype(jnp.float32) * (1.0 - learning * decay_rate) - learning * (
        first_next / first_fix
    ) / (jnp.sqrt(second_next / second_fix) + epsilon)
    return stepped.astype(jnp.bfloat16), first_next, second_next


def migrate_spread(arrays, source, experts):
    moved = []
    for array in arrays:
        split = array.reshape(experts, array.shape[0] // experts, array.shape[1])
        spread = lax.all_to_all(split, "expert", split_axis=0, concat_axis=0, tiled=True)
        ordered = jnp.take(spread, source, axis=0)
        home = lax.all_to_all(ordered, "expert", split_axis=0, concat_axis=0, tiled=True)
        moved.append(home.reshape(array.shape))
    return moved


def pack_tokens(token_block, route_block, gate_block, limit, wanted, capacity):
    valid = jnp.arange(token_block.shape[0], dtype=jnp.int32) < limit
    hits = (route_block[:, :, None] == wanted[None, None, :]) & valid[:, None, None]
    named = jnp.sum(hits.astype(jnp.int32), axis=1)
    scales = jnp.sum(jnp.where(hits, gate_block.astype(jnp.float32)[:, :, None], 0.0), axis=1)
    order = jnp.arange(token_block.shape[0], dtype=jnp.int32)
    earlier = (order[None, :] < order[:, None]).astype(jnp.bfloat16)
    ranks = jnp.dot(
        earlier, named.astype(jnp.bfloat16), preferred_element_type=jnp.float32
    ).astype(jnp.int32)
    slots = jnp.arange(capacity, dtype=jnp.int32)
    placed = (ranks.T[:, None, :] == slots[None, :, None]) & (named.T[:, None, :] == 1)
    scale = jnp.sum(jnp.where(placed, scales.T[:, None, :], 0.0), axis=2).astype(jnp.bfloat16)
    return placed.astype(jnp.bfloat16), scale


def exchange(array, experts, flip):
    return lax.ppermute(array, "expert", [(e, e ^ flip) for e in range(experts)])


def spread_in_plane(received, experts):
    blocks = []
    for step, own in enumerate(received):
        first, second = (1, 2) if step % 2 == 0 else (2, 1)
        near = exchange(own, experts, first)
        side = exchange(own, experts, second)
        far = exchange(near, experts, second)
        row = {0: own, first: near, second: side, 3: far}
        blocks.append([row[k] for k in range(GRP)])
    return blocks


def both_halves(mine, dp_size):
    if dp_size != 2:
        return lax.all_gather(mine, "dp", axis=0, tiled=True)
    other = lax.ppermute(mine, "dp", [(0, 1), (1, 0)])
    low = lax.axis_index("dp") == 0
    return jnp.concatenate([jnp.where(low, mine, other), jnp.where(low, other, mine)], axis=0)


def dot_t(acts, cot):
    return lax.dot_general(
        acts, cot, (((0,), (0,)), ((), ())), preferred_element_type=jnp.float32
    ).astype(jnp.bfloat16)


def summed_grads(acts, cot, rows_dev, dp_size):
    if dp_size != 2:
        return lax.psum_scatter(
            dot_t(acts, cot), "dp", scatter_dimension=0, tiled=True
        ).astype(jnp.float32)
    me = lax.axis_index("dp")
    theirs = dot_t(lax.dynamic_slice_in_dim(acts, (1 - me) * rows_dev, rows_dev, 1), cot)
    arrived = lax.ppermute(theirs, "dp", [(0, 1), (1, 0)])
    ours = dot_t(lax.dynamic_slice_in_dim(acts, me * rows_dev, rows_dev, 1), cot)
    return ours.astype(jnp.float32) + arrived.astype(jnp.float32)


def local(
    prev_acts,
    prev_cot,
    weights,
    first_moment,
    second_moment,
    tokens,
    routing,
    gates,
    token_counts,
    old_owner,
    new_owner,
):
    experts = lax.axis_size("expert")
    dp_size = lax.axis_size("dp")
    groups = experts // GRP
    token_slots = tokens.shape[2]
    capacity = min(token_slots, 3 * token_slots // groups)
    rows_dev, width = weights.shape[1:]
    hidden_units = width // 2
    hot_index = jnp.arange(groups, dtype=jnp.int32)
    holder = jnp.sum(
        jnp.where(new_owner[None, :] == hot_index[:, None], hot_index[None, :], 0), axis=1
    )
    came_from = jnp.take(old_owner, holder)
    my_group = lax.axis_index("expert") // GRP
    my_place = lax.axis_index("expert") % GRP

    placed, scale = pack_tokens(
        tokens[0, 0], routing[0, 0], gates[0, 0], token_counts[0, 0], holder, capacity
    )

    def finish(move, placed, scale, tokens, prev_acts, prev_cot, weights, first_moment, second_moment):
        received = []
        for step in range(groups):
            put = lax.dynamic_index_in_dim(placed, my_group ^ step, 0, keepdims=False)
            gate = lax.dynamic_index_in_dim(scale, my_group ^ step, 0, keepdims=False)
            rows = jnp.dot(put, tokens[0, 0], preferred_element_type=jnp.float32)
            packed = jnp.concatenate(
                [
                    rows.astype(jnp.bfloat16),
                    jnp.broadcast_to(gate[:, None], (capacity, LANES)),
                ],
                axis=1,
            )
            received.append(exchange(packed, experts, step * GRP) if step else packed)
        grads = summed_grads(prev_acts[0, 0], prev_cot[0, 0], rows_dev, dp_size)
        stepped, first_next, second_next = adamw(
            weights[0], first_moment[0], second_moment[0], grads
        )
        (new_weight,) = move(stepped)
        first_sent, second_sent, *received[1:] = lax.optimization_barrier(
            (first_next.astype(jnp.bfloat16), second_next.astype(jnp.bfloat16), *received[1:])
        )
        new_first, new_second = (
            array.astype(jnp.float32) for array in move(first_sent, second_sent)
        )
        blocks = spread_in_plane(received, experts)
        full = jnp.concatenate(
            [both_halves(new_weight, dp_size), jnp.zeros((LANES, width), jnp.bfloat16)], axis=0
        )
        rows = jnp.concatenate([block for row in blocks for block in row], axis=0)
        projected = jnp.dot(rows, full, preferred_element_type=jnp.float32)
        scale_in = rows[:, D]
        owners = jnp.arange(experts, dtype=jnp.int32)
        relative = owners ^ (my_group * GRP + my_place)
        projected = jnp.take(projected.reshape(experts, capacity, width), relative, axis=0)
        scale_in = jnp.take(scale_in.reshape(experts, capacity), relative, axis=0)
        result = (
            jax.nn.silu(projected[..., :hidden_units])
            * projected[..., hidden_units:]
            * scale_in.astype(jnp.float32)[:, :, None]
        )
        hidden = result.astype(jnp.bfloat16).reshape(1, 1, experts * capacity, hidden_units)
        return hidden, new_weight[None], new_first[None], new_second[None]

    operands = (placed, scale, tokens, prev_acts, prev_cot, weights, first_moment, second_moment)
    if groups > 4:
        owners = jnp.arange(experts, dtype=jnp.int32)
        source = jnp.take(came_from, owners // GRP) * GRP + owners % GRP

        def move(*arrays):
            return migrate_spread(arrays, source, experts)

        return finish(move, *operands)

    orders = list(itertools.permutations(range(groups)))

    def branch(order):
        pairs = [(order[e // GRP] * GRP + e % GRP, e) for e in range(experts)]

        def move(*arrays):
            if order == tuple(range(groups)):
                return arrays
            return [lax.ppermute(array, "expert", pairs) for array in arrays]

        return lambda *operands: finish(move, *operands)

    table = jnp.asarray(np.array(orders, np.int32))
    same = jnp.all(table == came_from[None, :], axis=1)
    chosen = jnp.sum(jnp.where(same, jnp.arange(len(orders), dtype=jnp.int32), 0))
    return lax.switch(chosen, [branch(order) for order in orders], *operands)


def solution(mesh):
    in_specs = (
        P("dp", "expert", None, None),
        P("dp", "expert", None, None),
        P("expert", "dp", None),
        P("expert", "dp", None),
        P("expert", "dp", None),
        P("dp", "expert", None, None),
        P("dp", "expert", None, None),
        P("dp", "expert", None, None),
        P("dp", "expert"),
        P(),
        P(),
    )
    out_specs = (
        P("dp", "expert", None, None),
        P("expert", "dp", None),
        P("expert", "dp", None),
        P("expert", "dp", None),
    )
    return jax.shard_map(local, mesh=mesh, in_specs=in_specs, out_specs=out_specs, check_vma=False)
```
